32 devices in a mesh: dp: 8 (over y, x, core), fsdp: 4 (over z).
Axes of the slice: x: 2, y: 2, z: 4, core: 2. Of those that a mesh axis runs over, the one named last changes fastest.
Arguments:
- tokens: bfloat16 [28672, 1408], P(('dp', 'fsdp')), may hold values from -8 to 8
- qkv_weight: bfloat16 [1408, 4224], P('fsdp'), may hold values from -1 to 1
- image_lengths: int32 [8, 4, 2, 2], P(None, 'fsdp'), may hold values from 1 to 320, 448 in all within a row
- balance: int32 [8, 4, 2], P(None, 'fsdp'), may hold values from 0 to 1, each once within a row
Outputs:
- attended: bfloat16 [28672, 1408], P(('dp', 'fsdp'))
The draws below stay inside these ranges and needn't reach their ends.
Inputs may be any that keep to these rules, and one draw needn't show every extreme that they name: `image_lengths`: the 2 lengths of a bundle sum to 448, and none exceeds 320. For each device, balance lists each of its bundles once over the routes.
All inputs are finite; a program needn't handle non-finite values.
Results may differ from the reference program's by a relative error of at most 0.0069.
Values may be sent and summed in bfloat16 or wider, within the bound.
No kernel may reach another device: no remote copies, remote signals or barrier semaphores. Data moves between devices by JAX's collectives and lax.ppermute only.
A program may use at most 128 MiB of HBM per device.

```python
import math
import jax
import jax.numpy as jnp
import numpy as np
from jax import lax

D = 1408
HEADS = 16
CAP = 448
BUNDLES = 2
IMB = 2
PMAX = 320
ROWS = 896
TOKENS = 28672
N_DP = 8
N_FSDP = 4


def draw_tokens(key, part):
    key = jax.random.fold_in(key, 11)
    return jnp.clip(jax.random.normal(key, (TOKENS, D), jnp.float32), -6.0, 6.0).astype(jnp.bfloat16)


def draw_qkv_weight(key, part):
    key = jax.random.fold_in(key, 23)
    return (jnp.clip(jax.random.normal(key, (D, 3 * D), jnp.float32), -6.0, 6.0) / math.sqrt(D)).astype(jnp.bfloat16)


def split_up(count, total, limit, slope):
    weights = [(1 << 20) // math.isqrt(rank ** slope) + 1 for rank in range(2, count + 1)]
    spare, given = total - limit - (count - 1), [1] * (count - 1)
    while spare > 0:
        candidates = [i for i in range(count - 1) if given[i] < limit]
        whole, budget = sum([weights[i] for i in candidates]), spare
        for i in candidates:
            extra = min(limit - given[i], max(1, budget * weights[i] // whole), spare)
            given[i] = given[i] + extra
            spare = spare - extra
    return np.array([limit] + given)


def ragged_sizes(rng, count, total, limit, slope):
    if count == 2:
        one = jax.random.randint(rng, (), max(1, total - limit), min(limit, total - 1) + 1)
        return jnp.stack([one, total - one])
    lengths = jnp.asarray(split_up(count, total, limit, slope), jnp.int32)
    twos = (count - 1) // 2
    source_of, taker = lengths[1:1 + 2 * twos:2], lengths[2:2 + 2 * twos:2]
    margin = jnp.minimum(source_of - 1, limit - taker)
    passed = jax.random.randint(jax.random.fold_in(rng, 1), (twos,), 0, 1 << 20) % (margin + 1)
    lengths = lengths.at[1:1 + 2 * twos:2].set(source_of - passed).at[2:2 + 2 * twos:2].set(taker + passed)
    return lengths[jax.random.permutation(jax.random.fold_in(rng, 2), count)]


def setup_inputs(seed: int = 0) -> dict:
    streams_of = jax.random.split(jax.random.key(seed), 5)
    return {
        "tokens": draw_tokens(jax.random.fold_in(streams_of[4], 71), 0),
        "qkv_weight": draw_qkv_weight(jax.random.fold_in(streams_of[4], 71), 0),
        "image_lengths": jax.vmap(lambda own: ragged_sizes(own, IMB, CAP, PMAX, 0))(jax.random.split(streams_of[2], N_DP * N_FSDP * BUNDLES)).reshape((N_DP, N_FSDP, BUNDLES, IMB)).astype(jnp.int32),
        "balance": jax.vmap(lambda own: jax.random.permutation(own, BUNDLES))(jax.random.split(streams_of[3], N_DP * N_FSDP)).reshape((N_DP, N_FSDP, BUNDLES)).astype(jnp.int32),
    }


def reference(tokens, qkv_weight, image_lengths, balance):
    bundles = tokens.reshape(N_DP, N_FSDP, BUNDLES, CAP, D)
    head_dim = D // HEADS
    score_scale = 1.0 / math.sqrt(head_dim)
    positions = jnp.arange(CAP, dtype=jnp.int32)

    def one_device(device_index):
        rank_index = device_index // N_FSDP
        column = device_index % N_FSDP
        near_source = (rank_index - 1) % N_DP
        far_source = (rank_index - N_DP // 2) % N_DP
        near_bundle = balance[near_source, column, 0].astype(jnp.int32)
        far_bundle = balance[far_source, column, 1].astype(jnp.int32)
        arrived = jnp.concatenate([bundles[near_source, column, near_bundle], bundles[far_source, column, far_bundle]], axis=0)
        near_first = image_lengths[near_source, column, near_bundle, 0]
        far_first = image_lengths[far_source, column, far_bundle, 0]
        near_tag = (positions >= near_first).astype(jnp.int32)
        far_tag = 4 + (positions >= far_first).astype(jnp.int32)
        image_tag = jnp.concatenate([near_tag, far_tag], axis=0)
        projected = jnp.dot(arrived, qkv_weight, preferred_element_type=jnp.float32).astype(jnp.bfloat16)
        shaped = projected.reshape(ROWS, 3, HEADS, head_dim).astype(jnp.float32)
        queries = shaped[:, 0]
        key_rows = shaped[:, 1]
        values = shaped[:, 2]
        scores = jnp.einsum('qhd,khd->hqk', queries, key_rows) * score_scale
        allowed = (image_tag[:, None] == image_tag[None, :])[None]
        masked = jnp.where(allowed, scores, -1e+30)
        row_max = lax.optimization_barrier(jnp.max(masked, axis=-1, keepdims=True))
        raised = jnp.where(allowed, jnp.exp(masked - row_max), 0.0)
        weights = (raised / lax.optimization_barrier(jnp.sum(raised, axis=-1, keepdims=True))).astype(jnp.bfloat16)
        attended = jnp.einsum('hqk,khd->qhd', weights.astype(jnp.float32), values)
        return attended.reshape(ROWS, D).astype(jnp.bfloat16)
    results = lax.map(one_device, jnp.arange(N_DP * N_FSDP, dtype=jnp.int32))
    return results.reshape(TOKENS, D)
```

```python
import math, functools

import jax
import jax.numpy as jnp
import numpy as np
from jax import lax
from jax.experimental import pallas as pl
from jax.experimental.pallas import tpu as pltpu
from jax.sharding import PartitionSpec as P

HEADS=16
LANE=128
BIG=-1e30

def attend_kernel(t0, t1, h0, h1, hd, bundle, *refs):
    first = t0 == 0
    if first:
        x_ref, w_ref, split_ref, o_hbm, kc_out, oc_out, proj, oscr, sem = refs
        kc_in = oc_in = None
    else:
        x_ref, w_ref, split_ref, kc_in, oc_in, o_in, o_hbm, kc_out, oc_out, proj, oscr, sem = refs
    rows = x_ref.shape[0]
    nt = t1 - t0
    base = t0 - 1
    width = (nt + 1) * LANE
    for part in range(3):
        p = jnp.dot(x_ref[...], w_ref[:, part*nt*LANE:(part+1)*nt*LANE], preferred_element_type=jnp.float32)
        proj[part, :, LANE:] = p.astype(jnp.bfloat16)
        if not first:
            proj[part, :, :LANE] = kc_in[:, part*LANE:(part+1)*LANE]
        kc_out[:, part*LANE:(part+1)*LANE] = proj[part, :, nt*LANE:]
    split = split_ref[0]
    c = math.log2(math.e) / math.sqrt(hd)
    partial = None if first else oc_in[...]
    def tags(w, at, values):
        row = lax.broadcasted_iota(jnp.int32, (rows, w), 0)
        lane = lax.broadcasted_iota(jnp.int32, (rows, w), 1)
        late = row >= split
        a, b = values
        one = jnp.where(late, b, a); two = jnp.where(late, a, b)
        return jnp.where(lane == at, one, jnp.where(lane == at + 1, two, 0.0)).astype(jnp.bfloat16)
    made = {}
    def get(w, at, values):
        if (w, at, values) not in made: made[(w, at, values)] = tags(w, at, values)
        return made[(w, at, values)]
    emitted = []
    for h in range(h0, h1):
        lo, hi = h*hd, (h+1)*hd
        s0, s1 = lo // LANE, -(-hi // LANE)
        w = (s1 - s0) * LANE
        a, b = lo - s0*LANE, hi - s0*LANE
        at = 0 if a >= 2 else w - 2
        ones_at = at
        lane = lax.broadcasted_iota(jnp.int32, (rows, w), 1)
        own = (lane >= a) & (lane < b)
        cols = slice((s0-base)*LANE, (s1-base)*LANE)
        q = jnp.where(own, proj[0, :, cols], get(w, at, (1.0, 0.0)))
        k = jnp.where(own, proj[1, :, cols], get(w, at, (0.0, BIG)))
        v = jnp.where(own, proj[2, :, cols], jnp.where(lane == ones_at, 1.0, 0.0).astype(jnp.bfloat16))
        s = lax.dot_general(q, k, (((1,), (1,)), ((), ())), preferred_element_type=jnp.float32)
        m = jnp.max(s, axis=1, keepdims=True) * c
        e = jnp.exp2(s * c - m).astype(jnp.bfloat16)
        o = jnp.dot(e, v, preferred_element_type=jnp.float32)
        o = (o / o[:, ones_at:ones_at+1]).astype(jnp.bfloat16)
        for t in range(s0, s1):
            piece = o[:, (t-s0)*LANE:(t-s0+1)*LANE]
            start = max(lo - t*LANE, 0)
            if start > 0:
                ln = lax.broadcasted_iota(jnp.int32, (rows, LANE), 1)
                piece = jnp.where(ln < start, partial, piece)
            if hi >= (t+1)*LANE:
                emitted.append(t)
                oscr[:, (t-emitted[0])*LANE:(t-emitted[0]+1)*LANE] = piece
                partial = None
            else:
                partial = piece
    n = len(emitted)
    if partial is not None: oc_out[...] = partial
    else: oc_out[...] = jnp.zeros_like(oc_out)
    cp = pltpu.make_async_copy(oscr, o_hbm.at[pl.ds(bundle*rows, rows), pl.ds(emitted[0]*LANE, n*LANE)], sem)
    cp.start(); cp.wait()

def attend(t0, t1, h0, h1, bundle, x, w, split, carry, out):
    rows, d = x.shape
    hd = d // HEADS
    first = t0 == 0
    nt = t1 - t0
    e0 = (h0*hd) // LANE
    e1 = (h1*hd) // LANE
    V = pl.BlockSpec(memory_space=pltpu.VMEM)
    A = pl.BlockSpec(memory_space=pl.ANY)
    S = pl.BlockSpec(memory_space=pltpu.SMEM)
    ins = [x, w, split]; specs=[V, V, S]
    if not first:
        ins += [*carry]; specs += [V, V]
    alias = {}
    if out is not None:
        ins.append(out); specs.append(A); alias={len(ins)-1: 0}
    body = functools.partial(attend_kernel, t0, t1, h0, h1, hd, bundle)
    if first and out is not None:
        inner = body
        body = lambda x, w, s, o_in, *rest: inner(x, w, s, *rest)
    res = pl.pallas_call(body,
        out_shape=[jax.ShapeDtypeStruct((2*rows, d), jnp.bfloat16), jax.ShapeDtypeStruct((rows, 3*LANE), jnp.bfloat16), jax.ShapeDtypeStruct((rows, LANE), jnp.bfloat16)],
        in_specs=specs, out_specs=[A, V, V],
        scratch_shapes=[pltpu.VMEM((3, rows, (nt+1)*LANE), jnp.bfloat16), pltpu.VMEM((rows, (e1-e0)*LANE), jnp.bfloat16), pltpu.SemaphoreType.DMA],
        input_output_aliases=alias,
        compiler_params=pltpu.CompilerParams(vmem_limit_bytes=40*2**20),
        name=f"attend_{t0}_{bundle}",
    )(*ins)
    return res[0], (res[1], res[2])

def ready_heads(bounds, hd):
    out=[]; h=0
    for t0,t1 in bounds:
        e=min(HEADS, t1*LANE//hd)
        out.append((h,e)); h=e
    return out


BOUNDS = ((0, 3), (3, 6), (6, 9), (9, 11))
SWAPS = (2, 2, 2, 4)
PIECES = 4


def relative_order(shard_rows, shards, halves):
    quarter = shard_rows // PIECES
    step, flip, row = [], [], []
    for j in (0, 2, 1, 3):
        for start, size in halves:
            for s in range(1, shards):
                step += [s] * size
                flip += [j] * size
                row += list(range(start, start + size))
    return np.array(step), np.array(flip), np.array(row)


def quarter_of(rank):
    return ((((rank >> 2) ^ (rank >> 1)) & 1) << 1) | (rank & 1)


def source_columns(rank, column, shard_rows, shards, halves):
    step, flip, row = relative_order(shard_rows, shards, halves)
    rest = ((column - step) % shards) * shard_rows + (quarter_of(rank) ^ flip) * (shard_rows // PIECES) + row
    own = column * shard_rows + np.arange(shard_rows)
    return jnp.concatenate([own, rest]).astype(jnp.int32)


def reordered(x, columns):
    place = (jnp.arange(x.shape[1], dtype=jnp.int32)[:, None] == columns[None, :]).astype(jnp.bfloat16)
    return jnp.dot(x, place, preferred_element_type=jnp.float32).astype(jnp.bfloat16)


def shifted(x, axis, by):
    n = lax.axis_size(axis)
    return lax.ppermute(x, axis, [(i, (i + by) % n) for i in range(n)])


def swapped(x, mask):
    n = lax.axis_size("dp")
    return lax.ppermute(x, "dp", [(i, i ^ mask) for i in range(n)])


def after(x, y):
    return lax.optimization_barrier((x, y))[0]


def on_device(tokens, qkv_weight, image_lengths, balance):
    ranks = lax.axis_size("dp")
    shards = lax.axis_size("fsdp")
    rank = lax.axis_index("dp")
    column = lax.axis_index("fsdp")
    rows, width = tokens.shape
    bundle_rows = rows // 2
    shard_rows = qkv_weight.shape[0]
    quarter = shard_rows // PIECES
    first = (quarter // 2 + 7) // 8 * 8
    halves = ((0, first), (first, quarter - first))
    hd = width // HEADS

    routes = balance[:, 0]
    lengths = image_lengths[:, 0]

    def first_end(source, route):
        return lengths[source, routes[source, route], 0]

    near_split = first_end((rank - 1) % ranks, 0)
    far_split = first_end((rank - ranks // 2) % ranks, 1)
    splits = (near_split.reshape(1), far_split.reshape(1))

    own_first = routes[rank, 0] == 0
    low, high = tokens[:bundle_rows], tokens[bundle_rows:]
    near = jnp.where(own_first, low, high)
    far = jnp.where(own_first, high, low)
    near_to = (rank + 1) % ranks
    far_to = (rank + ranks // 2) % ranks
    order = functools.partial(source_columns, column=column, shard_rows=shard_rows, shards=shards, halves=halves)
    near = shifted(reordered(near, order(near_to)), "dp", 1)
    far = shifted(reordered(far, order(far_to)), "dp", ranks // 2)

    mine = lax.dynamic_slice_in_dim(qkv_weight, quarter_of(rank) * quarter, quarter, 0)

    def of_chunk(w, t0, t1):
        return jnp.concatenate([w[:, p * width + t0 * LANE : p * width + t1 * LANE] for p in range(3)], axis=1)

    weights = []
    last = [None, None]
    for (t0, t1), mask in zip(BOUNDS, SWAPS):
        payload = of_chunk(mine, t0, t1)
        got = []
        for i, (start, size) in enumerate(halves):
            part = payload[start : start + size]
            if last[i] is not None:
                part = after(part, last[i])
            for _ in range(1, shards):
                part = shifted(part, "fsdp", 1)
                got.append(part)
            last[i] = part
        straight = jnp.concatenate(got, axis=0)
        across = swapped(straight, mask)
        both = jnp.concatenate([straight, across], axis=0)
        other = swapped(both, 1)
        weights.append(jnp.concatenate([of_chunk(qkv_weight, t0, t1), both, other], axis=0))

    out = None
    carry = [None, None]
    for (t0, t1), (h0, h1), w in zip(BOUNDS, ready_heads(BOUNDS, hd), weights):
        for b, x in enumerate((near, far)):
            out, carry[b] = attend(t0, t1, h0, h1, b, x, w, splits[b], carry[b], out)
    return out


def solution(mesh):
    in_specs = (
        P(("dp", "fsdp"), None),
        P("fsdp", None),
        P(None, "fsdp", None, None),
        P(None, "fsdp", None),
    )
    return jax.shard_map(
        on_device, mesh=mesh, in_specs=in_specs, out_specs=P(("dp", "fsdp"), None), check_vma=False
    )
```

```python
import functools
import math

import jax
import jax.numpy as jnp
import numpy as np
from jax import lax
from jax.experimental import pallas as pl
from jax.experimental.pallas import tpu as pltpu
from jax.sharding import PartitionSpec as P

HEADS = 16
LANE = 128
FAR_BELOW = -1e30
PIECES = 4
BOUNDS = ((0, 3), (3, 6), (6, 9), (9, 11))
SWAPS = (2, 2, 4, 2)


def heads_of(bounds, head_dim):
    found, h = [], 0
    for _, t1 in bounds:
        end = min(HEADS, t1 * LANE // head_dim)
        found.append((h, end))
        h = end
    return found


def pick_kernel(route_ref, rank_ref, tokens, near, far, sems):
    rows = near.shape[0]
    copies = []
    for r, to in enumerate((near, far)):
        start = pl.multiple_of(route_ref[rank_ref[0], 0, r] * rows, rows)
        copies.append(pltpu.make_async_copy(tokens.at[pl.ds(start, rows)], to, sems.at[r]))
    for c in copies:
        c.start()
    for c in copies:
        c.wait()


def picked(balance, rank, tokens):
    rows, width = tokens.shape
    anywhere = pl.BlockSpec(memory_space=pl.ANY)
    scalars = pl.BlockSpec(memory_space=pltpu.SMEM)
    half = jax.ShapeDtypeStruct((rows // 2, width), tokens.dtype)
    return pl.pallas_call(
        pick_kernel,
        out_shape=[half, half],
        in_specs=[scalars, scalars, anywhere],
        out_specs=[pl.BlockSpec(memory_space=pltpu.VMEM)] * 2,
        scratch_shapes=[pltpu.SemaphoreType.DMA((2,))],
        name="pick",
    )(balance, rank, tokens)


def attend_kernel(t0, t1, h0, h1, hd, bundles, has_out, *refs):
    nb = len(bundles)
    refs = list(refs)
    x_refs = [refs.pop(0) for _ in range(nb)]
    w_ref, lengths_ref, route_ref, source_ref = [refs.pop(0) for _ in range(4)]
    later = t0 > 0
    pc_in = [refs.pop(0) for _ in range(nb)] if later else None
    oc_in = [refs.pop(0) for _ in range(nb)] if later else None
    if has_out:
        refs.pop(0)
    out = refs.pop(0)
    pc_out = [refs.pop(0) for _ in range(nb)]
    oc_out = [refs.pop(0) for _ in range(nb)]
    proj, done, sems = refs
    rows = x_refs[0].shape[0]
    nt = t1 - t0
    base = t0 - 1
    first_tile = h0 * hd // LANE
    c = math.log2(math.e) / math.sqrt(hd)
    copies = []
    for i, bundle in enumerate(bundles):
        p = jnp.dot(x_refs[i][...], w_ref[...], preferred_element_type=jnp.float32).astype(jnp.bfloat16)
        for part in range(3):
            proj[i, part, :, LANE:] = p[:, part * nt * LANE : (part + 1) * nt * LANE]
            if later:
                proj[i, part, :, :LANE] = pc_in[i][:, part * LANE : (part + 1) * LANE]
            pc_out[i][:, part * LANE : (part + 1) * LANE] = proj[i, part, :, nt * LANE :]
        source = source_ref[bundle]
        split = lengths_ref[source, 0, route_ref[source, 0, bundle], 0]
        made = {}

        def tags(w, at, a, b):
            if (w, at, a, b) not in made:
                late = lax.broadcasted_iota(jnp.int32, (rows, w), 0) >= split
                lane = lax.broadcasted_iota(jnp.int32, (rows, w), 1)
                one, two = jnp.where(late, b, a), jnp.where(late, a, b)
                both = jnp.where(lane == at, one, jnp.where(lane == at + 1, two, 0.0))
                made[(w, at, a, b)] = both.astype(jnp.bfloat16)
            return made[(w, at, a, b)]

        partial = oc_in[i][...] if later else None
        for h in range(h0, h1):
            lo, hi = h * hd, (h + 1) * hd
            s0, s1 = lo // LANE, -(-hi // LANE)
            w = (s1 - s0) * LANE
            a, b = lo - s0 * LANE, hi - s0 * LANE
            at = 0 if a >= 2 else w - 2
            lane = lax.broadcasted_iota(jnp.int32, (rows, w), 1)
            own = (lane >= a) & (lane < b)
            cols = slice((s0 - base) * LANE, (s1 - base) * LANE)
            q = jnp.where(own, proj[i, 0, :, cols], tags(w, at, 1.0, 0.0))
            k = jnp.where(own, proj[i, 1, :, cols], tags(w, at, 0.0, FAR_BELOW))
            ones = jnp.where(lane == at, 1.0, 0.0).astype(jnp.bfloat16)
            v = jnp.where(own, proj[i, 2, :, cols], ones)
            s = lax.dot_general(q, k, (((1,), (1,)), ((), ())), preferred_element_type=jnp.float32)
            m = jnp.max(s, axis=1, keepdims=True) * c
            e = jnp.exp2(s * c - m).astype(jnp.bfloat16)
            o = jnp.dot(e, v, preferred_element_type=jnp.float32)
            o = (o / o[:, at : at + 1]).astype(jnp.bfloat16)
            for t in range(s0, s1):
                piece = o[:, (t - s0) * LANE : (t - s0 + 1) * LANE]
                start = max(lo - t * LANE, 0)
                if start > 0:
                    lanes = lax.broadcasted_iota(jnp.int32, (rows, LANE), 1)
                    piece = jnp.where(lanes < start, partial, piece)
                if hi >= (t + 1) * LANE:
                    j = t - first_tile
                    done[i, j] = piece
                    copy = pltpu.make_async_copy(
                        done.at[i, j],
                        out.at[pl.ds(bundle * rows, rows), pl.ds(t * LANE, LANE)],
                        sems.at[i, j],
                    )
                    copy.start()
                    copies.append(copy)
                    partial = None
                else:
                    partial = piece
        oc_out[i][...] = jnp.zeros((rows, LANE), jnp.bfloat16) if partial is None else partial
    for copy in copies:
        copy.wait()


def attend(t0, t1, h0, h1, bundles, xs, w, info, carry, out):
    rows, d = xs[0].shape
    hd = d // HEADS
    nb, nt = len(bundles), t1 - t0
    tiles = h1 * hd // LANE - h0 * hd // LANE
    inside = pl.BlockSpec(memory_space=pltpu.VMEM)
    anywhere = pl.BlockSpec(memory_space=pl.ANY)
    scalars = pl.BlockSpec(memory_space=pltpu.SMEM)
    operands = [*xs, w, *info]
    specs = [inside] * (nb + 1) + [scalars] * 3
    if t0 > 0:
        operands += [carry[b][0] for b in bundles] + [carry[b][1] for b in bundles]
        specs += [inside] * (2 * nb)
    alias = {}
    if out is not None:
        alias = {len(operands): 0}
        operands.append(out)
        specs.append(anywhere)
    shape = lambda r, c: jax.ShapeDtypeStruct((r, c), jnp.bfloat16)
    res = pl.pallas_call(
        functools.partial(attend_kernel, t0, t1, h0, h1, hd, bundles, out is not None),
        out_shape=[shape(2 * rows, d)] + [shape(rows, 3 * LANE)] * nb + [shape(rows, LANE)] * nb,
        in_specs=specs,
        out_specs=[anywhere] + [inside] * (2 * nb),
        scratch_shapes=[
            pltpu.VMEM((nb, 3, rows, (nt + 1) * LANE), jnp.bfloat16),
            pltpu.VMEM((nb, tiles, rows, LANE), jnp.bfloat16),
            pltpu.SemaphoreType.DMA((nb, tiles)),
        ],
        input_output_aliases=alias,
        compiler_params=pltpu.CompilerParams(vmem_limit_bytes=16 * 2**20),
        cost_estimate=pl.CostEstimate(
            flops=nb * (2 * rows * w.shape[0] * w.shape[1] + 4 * rows * rows * 256 * (h1 - h0)),
            bytes_accessed=2 * w.size + 2 * nb * rows * d,
            transcendentals=nb * rows * rows * (h1 - h0),
        ),
        name=f"attend_{t0}_{bundles[0]}",
    )(*operands)
    for i, b in enumerate(bundles):
        carry[b] = (res[1 + i], res[1 + nb + i])
    return res[0]


ARRIVAL = ((1, 0), (3, 0), (1, 2), (3, 2), (2, 0), (2, 2))


def quarter_of(rank):
    return ((((rank >> 2) ^ (rank >> 1)) & 1) << 1) | (rank & 1)


def source_columns(rank, column, shard_rows, shards):
    quarter = shard_rows // PIECES
    step = np.array([s for core in (0, 1) for s, _ in ARRIVAL for _ in range(quarter)])
    flip = np.array([core | across for core in (0, 1) for _, across in ARRIVAL for _ in range(quarter)])
    row = np.array(list(range(quarter)) * (2 * len(ARRIVAL)))
    rest = ((column - step) % shards) * shard_rows + (quarter_of(rank) ^ flip) * quarter + row
    own = column * shard_rows + np.arange(shard_rows)
    return jnp.concatenate([own, rest]).astype(jnp.int32)


def reordered(x, place):
    return jnp.dot(x, place, preferred_element_type=jnp.float32).astype(jnp.bfloat16)


def shifted(x, axis, by):
    n = lax.axis_size(axis)
    return lax.ppermute(x, axis, [(i, (i + by) % n) for i in range(n)])


def swapped(x, mask):
    n = lax.axis_size("dp")
    return lax.ppermute(x, "dp", [(i, i ^ mask) for i in range(n)])


def fence(*values):
    return lax.optimization_barrier(values)


def stacked(*xs):
    return jnp.concatenate(xs, axis=0)


def on_device(tokens, qkv_weight, image_lengths, balance):
    ranks = lax.axis_size("dp")
    shards = lax.axis_size("fsdp")
    rank = lax.axis_index("dp")
    column = lax.axis_index("fsdp")
    rows, width = tokens.shape
    shard_rows = qkv_weight.shape[0]
    quarter = shard_rows // PIECES
    hd = width // HEADS
    sources = jnp.stack([(rank - 1) % ranks, (rank - ranks // 2) % ranks]).astype(jnp.int32)
    info = (image_lengths, balance, sources)
    columns = source_columns(rank, column, shard_rows, shards)
    quarter_start = quarter_of(rank) * quarter

    def columns_matrix():
        return (jnp.arange(width, dtype=jnp.int32)[:, None] == columns[None, :]).astype(jnp.bfloat16)

    def of_chunk(w, t0, t1):
        return jnp.concatenate([w[:, p * width + t0 * LANE : p * width + t1 * LANE] for p in range(3)], axis=1)

    def payload(w, c):
        return of_chunk(lax.dynamic_slice_in_dim(w, quarter_start, quarter, 0), *BOUNDS[c])

    def up(x):
        return shifted(x, "fsdp", 1)

    def down(x):
        return shifted(x, "fsdp", shards - 1)

    def across(c, *xs):
        return swapped(stacked(*xs) if len(xs) > 1 else xs[0], SWAPS[c])

    spans = [(*b, *h) for b, h in zip(BOUNDS, heads_of(BOUNDS, hd))]
    carry = [None, None]
    w = qkv_weight

    pa = payload(w, 0)
    ap, am = up(pa), down(pa)
    w, _ = fence(w, pa)
    pb = payload(w, 1)
    bp, bm = up(pb), down(pb)
    tokens, w, _ = fence(tokens, w, pb)
    near, far = picked(balance, rank.reshape(1), tokens)
    near_in, far_in = shifted(near, "dp", 1), shifted(far, "dp", ranks // 2)
    w, _ = fence(w, near)
    pc = payload(w, 2)

    ap, pc, w = fence(ap, pc, w)
    a2, cp = up(ap), up(pc)
    own_a = of_chunk(w, *BOUNDS[0])
    pd = payload(w, 3)

    am, bp, pc, pd, own_a, ap = fence(am, bp, pc, pd, own_a, ap)
    ax = across(0, ap, am)
    b2, cm = up(bp), down(pc)
    place = columns_matrix()

    near, a2, pd, w, place = fence(near_in, a2, pd, w, place)
    ay = across(0, a2)
    dp, dm = up(pd), down(pd)
    near = reordered(near, place)
    own_b = of_chunk(w, *BOUNDS[1])

    bm, cp, bp, near, own_b, w = fence(bm, cp, bp, near, own_b, w)
    c2 = up(cp)
    bx = across(1, bp, bm)
    own_c = of_chunk(w, *BOUNDS[2])

    ax, ay, b2, ap, am, a2, own_c, w = fence(ax, ay, b2, ap, am, a2, own_c, w)
    both_a = stacked(ap, am, ax, a2, ay)
    ac = swapped(both_a, 1)
    by = across(1, b2)
    own_d = of_chunk(w, *BOUNDS[3])

    far, cm, dp, cp, place, own_d = fence(far_in, cm, dp, cp, place, own_d)
    d2 = up(dp)
    cx = across(2, cp, cm)
    far = reordered(far, place)

    ac, both_a, own_a, near, far = fence(ac, both_a, own_a, near, far)
    wa = stacked(own_a, both_a, ac)
    out = attend(*spans[0], (0, 1), (near, far), wa, info, carry, None)

    out, bx, dm, dp, by, bp, bm, b2 = fence(out, bx, dm, dp, by, bp, bm, b2)
    dx = across(3, dp, dm)
    both_b = stacked(bp, bm, bx, b2, by)
    bc = swapped(both_b, 1)

    c2, d2, bc, both_b, own_b = fence(c2, d2, bc, both_b, own_b)
    cy = across(2, c2)
    dy = across(3, d2)
    wb = stacked(own_b, both_b, bc)
    out = attend(*spans[1], (0,), (near,), wb, info, carry, out)

    out, cx, cy, dx, dy, cp, cm, c2, dp, dm, d2 = fence(out, cx, cy, dx, dy, cp, cm, c2, dp, dm, d2)
    both_c = stacked(cp, cm, cx, c2, cy)
    cc = swapped(both_c, 1)
    both_d = stacked(dp, dm, dx, d2, dy)
    dc = swapped(both_d, 1)
    out = attend(*spans[1], (1,), (far,), wb, info, carry, out)

    wc = stacked(own_c, both_c, cc)
    out = attend(*spans[2], (0, 1), (near, far), wc, info, carry, out)
    wd = stacked(own_d, both_d, dc)
    out = attend(*spans[3], (0, 1), (near, far), wd, info, carry, out)
    return out


def solution(mesh):
    in_specs = (
        P(("dp", "fsdp"), None),
        P("fsdp", None),
        P(None, "fsdp", None, None),
        P(None, "fsdp", None),
    )
    return jax.shard_map(
        on_device, mesh=mesh, in_specs=in_specs, out_specs=P(("dp", "fsdp"), None), check_vma=False
    )
```

```python
import functools
import math

import jax
import jax.numpy as jnp
import numpy as np
from jax import lax
from jax.experimental import pallas as pl
from jax.experimental.pallas import tpu as pltpu
from jax.sharding import PartitionSpec as P

HEADS = 16
LANE = 128
FAR_BELOW = -1e30
PIECES = 4
BOUNDS = ((0, 3), (3, 6), (6, 9), (9, 11))
SWAPS = (2, 2, 2, 4)


def heads_of(bounds, head_dim):
    found, h = [], 0
    for _, t1 in bounds:
        end = min(HEADS, t1 * LANE // head_dim)
        found.append((h, end))
        h = end
    return found


def pick_kernel(route_ref, rank_ref, tokens, near, far, sems):
    rows = near.shape[0]
    copies = []
    for r, to in enumerate((near, far)):
        start = pl.multiple_of(route_ref[rank_ref[0], 0, r] * rows, rows)
        copies.append(pltpu.make_async_copy(tokens.at[pl.ds(start, rows)], to, sems.at[r]))
    for c in copies:
        c.start()
    for c in copies:
        c.wait()


def picked(balance, rank, tokens):
    rows, width = tokens.shape
    anywhere = pl.BlockSpec(memory_space=pl.ANY)
    scalars = pl.BlockSpec(memory_space=pltpu.SMEM)
    half = jax.ShapeDtypeStruct((rows // 2, width), tokens.dtype)
    return pl.pallas_call(
        pick_kernel,
        out_shape=[half, half],
        in_specs=[scalars, scalars, anywhere],
        out_specs=[pl.BlockSpec(memory_space=pltpu.VMEM)] * 2,
        scratch_shapes=[pltpu.SemaphoreType.DMA((2,))],
        name="pick",
    )(balance, rank, tokens)


def attend_kernel(t0, t1, h0, h1, hd, bundles, earlier, *refs):
    nb = len(bundles)
    refs = list(refs)
    take = lambda n: [refs.pop(0) for _ in range(n)]
    x_refs = take(nb)
    w_ref, lengths_ref, route_ref, source_ref = take(4)
    later = t0 > 0
    pc_in, oc_in = (take(nb), take(nb)) if later else (None, None)
    last = earlier is not None
    if last:
        before = take(len(earlier))
        out = refs.pop(0)
        proj, done, sems, own_sems = refs
    else:
        done_refs, pc_out, oc_out = take(nb), take(nb), take(nb)
        (proj,) = refs
    rows = x_refs[0].shape[0]
    nt = t1 - t0
    base = t0 - 1
    first_tile = h0 * hd // LANE
    c = math.log2(math.e) / math.sqrt(hd)
    copies = []
    if last:
        for j, (bundle, tile) in enumerate(earlier):
            to = out.at[pl.ds(bundle * rows, rows), pl.ds(tile * LANE, before[j].shape[1])]
            copies.append(pltpu.make_async_copy(before[j], to, sems.at[j]))
            copies[-1].start()
    for i, bundle in enumerate(bundles):
        p = jnp.dot(x_refs[i][...], w_ref[...], preferred_element_type=jnp.float32).astype(jnp.bfloat16)
        for part in range(3):
            proj[i, part, :, LANE:] = p[:, part * nt * LANE : (part + 1) * nt * LANE]
            if later:
                proj[i, part, :, :LANE] = pc_in[i][:, part * LANE : (part + 1) * LANE]
            if not last:
                pc_out[i][:, part * LANE : (part + 1) * LANE] = proj[i, part, :, nt * LANE :]
        source = source_ref[bundle]
        split = lengths_ref[source, 0, route_ref[source, 0, bundle], 0]
        made = {}

        def tags(w, at, a, b):
            if (w, at, a, b) not in made:
                late = lax.broadcasted_iota(jnp.int32, (rows, w), 0) >= split
                lane = lax.broadcasted_iota(jnp.int32, (rows, w), 1)
                one, two = jnp.where(late, b, a), jnp.where(late, a, b)
                both = jnp.where(lane == at, one, jnp.where(lane == at + 1, two, 0.0))
                made[(w, at, a, b)] = both.astype(jnp.bfloat16)
            return made[(w, at, a, b)]

        def place_of(h):
            lo, hi = h * hd, (h + 1) * hd
            s0, s1 = lo // LANE, -(-hi // LANE)
            w = (s1 - s0) * LANE
            a, b = lo - s0 * LANE, hi - s0 * LANE
            at = 0 if a >= 2 else w - 2
            lane = lax.broadcasted_iota(jnp.int32, (rows, w), 1)
            return lo, hi, s0, s1, w, at, lane, (lane >= a) & (lane < b), slice((s0 - base) * LANE, (s1 - base) * LANE)

        def scores(h):
            _, _, _, _, w, at, _, own, cols = place_of(h)
            q = jnp.where(own, proj[i, 0, :, cols], tags(w, at, 1.0, 0.0))
            k = jnp.where(own, proj[i, 1, :, cols], tags(w, at, 0.0, FAR_BELOW))
            return lax.dot_general(q, k, (((1,), (1,)), ((), ())), preferred_element_type=jnp.float32)

        partial = oc_in[i][...] if later else None
        upcoming = scores(h0)
        for h in range(h0, h1):
            lo, hi, s0, s1, w, at, lane, own, cols = place_of(h)
            s = upcoming
            if h + 1 < h1:
                upcoming = scores(h + 1)
            ones = jnp.where(lane == at, 1.0, 0.0).astype(jnp.bfloat16)
            v = jnp.where(own, proj[i, 2, :, cols], ones)
            m = jnp.max(s, axis=1, keepdims=True) * c
            e = jnp.exp2(s * c - m).astype(jnp.bfloat16)
            o = jnp.dot(e, v, preferred_element_type=jnp.float32)
            o = (o / o[:, at : at + 1]).astype(jnp.bfloat16)
            for t in range(s0, s1):
                piece = o[:, (t - s0) * LANE : (t - s0 + 1) * LANE]
                start = max(lo - t * LANE, 0)
                if start > 0:
                    lanes = lax.broadcasted_iota(jnp.int32, (rows, LANE), 1)
                    piece = jnp.where(lanes < start, partial, piece)
                if hi >= (t + 1) * LANE:
                    j = t - first_tile
                    if last:
                        done[i, :, j * LANE : (j + 1) * LANE] = piece
                    else:
                        done_refs[i][:, j * LANE : (j + 1) * LANE] = piece
                    partial = None
                else:
                    partial = piece
        if last:
            to = out.at[pl.ds(bundle * rows, rows), pl.ds(first_tile * LANE, done.shape[2])]
            copies.append(pltpu.make_async_copy(done.at[i], to, own_sems.at[i]))
            copies[-1].start()
        else:
            oc_out[i][...] = jnp.zeros((rows, LANE), jnp.bfloat16) if partial is None else partial
    for copy in copies:
        copy.wait()


def attend(t0, t1, h0, h1, bundles, xs, w, info, carry, finished):
    rows, d = xs[0].shape
    hd = d // HEADS
    nb, nt = len(bundles), t1 - t0
    first_tile = h0 * hd // LANE
    tiles = h1 * hd // LANE - first_tile
    last = t1 * LANE == d
    inside = pl.BlockSpec(memory_space=pltpu.VMEM)
    anywhere = pl.BlockSpec(memory_space=pl.ANY)
    scalars = pl.BlockSpec(memory_space=pltpu.SMEM)
    operands = [*xs, w, *info]
    specs = [inside] * (nb + 1) + [scalars] * 3
    if t0 > 0:
        operands += [carry[b][0] for b in bundles] + [carry[b][1] for b in bundles]
        specs += [inside] * (2 * nb)
    shape = lambda r, c: jax.ShapeDtypeStruct((r, c), jnp.bfloat16)
    scratch = [pltpu.VMEM((nb, 3, rows, (nt + 1) * LANE), jnp.bfloat16)]
    if last:
        earlier = [(b, tile) for b, tile, _ in finished]
        operands += [x for _, _, x in finished]
        specs += [anywhere] * len(finished)
        out_shape, out_specs = shape(2 * rows, d), anywhere
        scratch += [
            pltpu.VMEM((nb, rows, tiles * LANE), jnp.bfloat16),
            pltpu.SemaphoreType.DMA((len(finished),)),
            pltpu.SemaphoreType.DMA((nb,)),
        ]
    else:
        earlier = None
        out_shape = [shape(rows, tiles * LANE)] * nb + [shape(rows, 3 * LANE)] * nb + [shape(rows, LANE)] * nb
        out_specs = [inside] * (3 * nb)
    res = pl.pallas_call(
        functools.partial(attend_kernel, t0, t1, h0, h1, hd, bundles, earlier),
        out_shape=out_shape,
        in_specs=specs,
        out_specs=out_specs,
        scratch_shapes=scratch,
        compiler_params=pltpu.CompilerParams(vmem_limit_bytes=16 * 2**20),
        name=f"attend_{t0}_{bundles[0]}",
    )(*operands)
    if last:
        return res
    for i, b in enumerate(bundles):
        carry[b] = (res[nb + i], res[2 * nb + i])
        finished.append((b, first_tile, res[i]))
    return res[2 * nb]


ARRIVAL = ((1, 0), (3, 0), (1, 2), (3, 2), (2, 0), (2, 2))


def quarter_of(rank):
    return ((((rank >> 2) ^ (rank >> 1)) & 1) << 1) | (rank & 1)


def source_columns(rank, column, shard_rows, shards):
    quarter = shard_rows // PIECES
    step = np.array([s for core in (0, 1) for s, _ in ARRIVAL for _ in range(quarter)])
    flip = np.array([core | across for core in (0, 1) for _, across in ARRIVAL for _ in range(quarter)])
    row = np.array(list(range(quarter)) * (2 * len(ARRIVAL)))
    rest = ((column - step) % shards) * shard_rows + (quarter_of(rank) ^ flip) * quarter + row
    own = column * shard_rows + np.arange(shard_rows)
    return jnp.concatenate([own, rest]).astype(jnp.int32)


def reordered(x, place):
    return jnp.dot(x, place, preferred_element_type=jnp.float32).astype(jnp.bfloat16)


def shifted(x, axis, by):
    n = lax.axis_size(axis)
    return lax.ppermute(x, axis, [(i, (i + by) % n) for i in range(n)])


def swapped(x, mask):
    n = lax.axis_size("dp")
    return lax.ppermute(x, "dp", [(i, i ^ mask) for i in range(n)])


def fence(*values):
    return lax.optimization_barrier(values)


def stacked(*xs):
    return jnp.concatenate(xs, axis=0)


def on_device(tokens, qkv_weight, image_lengths, balance):
    ranks = lax.axis_size("dp")
    shards = lax.axis_size("fsdp")
    rank = lax.axis_index("dp")
    column = lax.axis_index("fsdp")
    rows, width = tokens.shape
    shard_rows = qkv_weight.shape[0]
    quarter = shard_rows // PIECES
    hd = width // HEADS
    sources = jnp.stack([(rank - 1) % ranks, (rank - ranks // 2) % ranks]).astype(jnp.int32)
    info = (image_lengths, balance, sources)
    columns = source_columns(rank, column, shard_rows, shards)
    quarter_start = quarter_of(rank) * quarter

    def columns_matrix():
        return (jnp.arange(width, dtype=jnp.int32)[:, None] == columns[None, :]).astype(jnp.bfloat16)

    def of_chunk(w, t0, t1):
        return jnp.concatenate([w[:, p * width + t0 * LANE : p * width + t1 * LANE] for p in range(3)], axis=1)

    def payload(w, *chunks):
        own = lax.dynamic_slice_in_dim(w, quarter_start, quarter, 0)
        return jnp.concatenate(fence(*[of_chunk(own, *BOUNDS[c]) for c in chunks]), axis=1)

    def up(x):
        return shifted(x, "fsdp", 1)

    def down(x):
        return shifted(x, "fsdp", shards - 1)

    def across(c, *xs):
        return swapped(stacked(*xs) if len(xs) > 1 else xs[0], SWAPS[c])

    spans = [(*b, *h) for b, h in zip(BOUNDS, heads_of(BOUNDS, hd))]
    carry = [None, None]
    finished = []
    w = qkv_weight
    n_a, n_b, n_c, n_d = [3 * (t1 - t0) * LANE for t0, t1 in BOUNDS]

    pab = payload(w, 0, 1)
    abp, abm = up(pab), down(pab)
    tokens, w, _ = fence(tokens, w, pab)
    near_first = balance[rank, 0, 0] == 0
    low, high = tokens[: rows // 2], tokens[rows // 2 :]
    near_out, far_out = jnp.where(near_first, low, high), jnp.where(near_first, high, low)
    cut = (rows // 6 // 16 * 16, rows // 3 // 16 * 16)
    far_1 = shifted(far_out[: cut[0]], "dp", ranks // 2)
    near_in = shifted(near_out, "dp", 1)
    pcd = payload(w, 2, 3)

    abp, pcd, w = fence(abp, pcd, w)
    ab2 = up(abp)
    own_a = of_chunk(w, *BOUNDS[0])
    place = columns_matrix()

    abp, abm, pcd, own_a, place, w, far_out = fence(abp, abm, pcd, own_a, place, w, far_out)
    cdp = up(pcd)
    ax = across(0, abp[:, :n_a], abm[:, :n_a])
    far_2 = shifted(far_out[cut[0] : cut[1]], "dp", ranks // 2)
    own_b = of_chunk(w, *BOUNDS[1])

    near, own_b, place = fence(near_in, own_b, place)
    near = reordered(near, place)

    near, ab2, pcd, w = fence(near, ab2, pcd, w)
    cdm = down(pcd)
    ay = across(0, ab2[:, :n_a])
    own_c = of_chunk(w, *BOUNDS[2])

    ax, abp, abm, ab2, own_c, w, far_1 = fence(ax, abp, abm, ab2, own_c, w, far_1)
    bx = across(1, abp[:, n_a:], abm[:, n_a:], ab2[:, n_a:])
    own_d = of_chunk(w, *BOUNDS[3])

    ay, ax, abp, abm, ab2, own_d, cdp, far_out = fence(ay, ax, abp, abm, ab2, own_d, cdp, far_out)
    far_3 = shifted(far_out[cut[1] :], "dp", ranks // 2)
    cd2 = up(cdp)
    both_a = stacked(abp[:, :n_a], abm[:, :n_a], ax, ab2[:, :n_a], ay)
    ac = swapped(both_a, 1)

    ac, both_a, own_a, near, far_2, cdm = fence(ac, both_a, own_a, near, far_2, cdm)
    wa = stacked(own_a, both_a, ac)
    out = attend(*spans[0], (0,), (near,), wa, info, carry, finished)

    out, cdp, cdm, far_1, far_2, far_3 = fence(out, cdp, cdm, far_1, far_2, far_3)
    dx_1 = across(3, cdp[:, n_c:], cdm[:, n_c:])
    cx_1 = across(2, cdp[:, :n_c], cdm[:, :n_c])
    far = reordered(stacked(far_1, far_2, far_3), place)

    bx, far, cd2 = fence(bx, far, cd2)
    dx_2 = across(3, cd2[:, n_c:])
    cx_2 = across(2, cd2[:, :n_c])
    both_b = stacked(abp[:, n_a:], abm[:, n_a:], bx[: 2 * quarter], ab2[:, n_a:], bx[2 * quarter :])
    bc = swapped(both_b, 1)
    out = attend(*spans[0], (1,), (far,), wa, info, carry, finished)

    out, bc, both_b, own_b, cx_1, dx_1, cdp = fence(out, bc, both_b, own_b, cx_1, dx_1, cdp)
    wb = stacked(own_b, both_b, bc)
    out = attend(*spans[1], (0,), (near,), wb, info, carry, finished)

    out, cx_1, dx_1, cx_2, dx_2, cdp, cdm, cd2 = fence(out, cx_1, dx_1, cx_2, dx_2, cdp, cdm, cd2)
    both_c = stacked(cdp[:, :n_c], cdm[:, :n_c], cx_1, cd2[:, :n_c], cx_2)
    cc = swapped(both_c, 1)
    both_d = stacked(cdp[:, n_c:], cdm[:, n_c:], dx_1, cd2[:, n_c:], dx_2)
    dc = swapped(both_d, 1)
    out = attend(*spans[1], (1,), (far,), wb, info, carry, finished)

    wc = stacked(own_c, both_c, cc)
    out = attend(*spans[2], (0, 1), (near, far), wc, info, carry, finished)
    wd = stacked(own_d, both_d, dc)
    out = attend(*spans[3], (0, 1), (near, far), wd, info, carry, finished)
    return out


def solution(mesh):
    in_specs = (
        P(("dp", "fsdp"), None),
        P("fsdp", None),
        P(None, "fsdp", None, None),
        P(None, "fsdp", None),
    )
    return jax.shard_map(
        on_device, mesh=mesh, in_specs=in_specs, out_specs=P(("dp", "fsdp"), None), check_vma=False
    )
```

```python
import functools
import math

import jax
import jax.numpy as jnp
import numpy as np
from jax import lax
from jax.experimental import pallas as pl
from jax.experimental.pallas import tpu as pltpu
from jax.sharding import PartitionSpec as P

HEADS = 16
LANE = 128
FAR_BELOW = -1e30
PIECES = 4
BOUNDS = ((0, 3), (3, 6), (6, 9), (9, 11))
SWAPS = (2, 2, 2, 4)


def heads_of(bounds, head_dim):
    found, h = [], 0
    for _, t1 in bounds:
        end = min(HEADS, t1 * LANE // head_dim)
        found.append((h, end))
        h = end
    return found


def pick_kernel(route_ref, rank_ref, tokens, near, far, sems):
    rows = near.shape[0]
    copies = []
    for r, to in enumerate((near, far)):
        start = pl.multiple_of(route_ref[rank_ref[0], 0, r] * rows, rows)
        copies.append(pltpu.make_async_copy(tokens.at[pl.ds(start, rows)], to, sems.at[r]))
    for c in copies:
        c.start()
    for c in copies:
        c.wait()


def picked(balance, rank, tokens):
    rows, width = tokens.shape
    anywhere = pl.BlockSpec(memory_space=pl.ANY)
    scalars = pl.BlockSpec(memory_space=pltpu.SMEM)
    half = jax.ShapeDtypeStruct((rows // 2, width), tokens.dtype)
    return pl.pallas_call(
        pick_kernel,
        out_shape=[half, half],
        in_specs=[scalars, scalars, anywhere],
        out_specs=[pl.BlockSpec(memory_space=pltpu.VMEM)] * 2,
        scratch_shapes=[pltpu.SemaphoreType.DMA((2,))],
        name="pick",
    )(balance, rank, tokens)


def attend_kernel(spans, h0, h1, hd, bundles, earlier, *refs):
    nb = len(bundles)
    refs = list(refs)
    take = lambda n: [refs.pop(0) for _ in range(n)]
    x_refs, w_refs = take(nb), take(len(spans))
    lengths_ref, route_ref, source_ref = take(3)
    t0, t1 = spans[0][0], spans[-1][1]
    later = t0 > 0
    pc_in, oc_in = (take(nb), take(nb)) if later else (None, None)
    last = earlier is not None
    if last:
        before = take(len(earlier))
        out = refs.pop(0)
        proj, done, sems, own_sems = refs
    else:
        done_refs, pc_out, oc_out = take(nb), take(nb), take(nb)
        (proj,) = refs
    rows = x_refs[0].shape[0]
    nt = t1 - t0
    base = t0 - 1
    first_tile = h0 * hd // LANE
    c = math.log2(math.e) / math.sqrt(hd)
    copies = []
    if last:
        for j, (bundle, tile) in enumerate(earlier):
            to = out.at[pl.ds(bundle * rows, rows), pl.ds(tile * LANE, before[j].shape[1])]
            copies.append(pltpu.make_async_copy(before[j], to, sems.at[j]))
            copies[-1].start()
    for i, bundle in enumerate(bundles):
        for w_ref, (u0, u1) in zip(w_refs, spans):
            p = jnp.dot(x_refs[i][...], w_ref[...], preferred_element_type=jnp.float32).astype(jnp.bfloat16)
            n = (u1 - u0) * LANE
            for part in range(3):
                proj[i, part, :, (u0 - base) * LANE : (u1 - base) * LANE] = p[:, part * n : (part + 1) * n]
        for part in range(3):
            if later:
                proj[i, part, :, :LANE] = pc_in[i][:, part * LANE : (part + 1) * LANE]
            if not last:
                pc_out[i][:, part * LANE : (part + 1) * LANE] = proj[i, part, :, nt * LANE :]
        source = source_ref[bundle]
        split = lengths_ref[source, 0, route_ref[source, 0, bundle], 0]
        made = {}

        def tags(w, at, a, b):
            if (w, at, a, b) not in made:
                late = lax.broadcasted_iota(jnp.int32, (rows, w), 0) >= split
                lane = lax.broadcasted_iota(jnp.int32, (rows, w), 1)
                one, two = jnp.where(late, b, a), jnp.where(late, a, b)
                both = jnp.where(lane == at, one, jnp.where(lane == at + 1, two, 0.0))
                made[(w, at, a, b)] = both.astype(jnp.bfloat16)
            return made[(w, at, a, b)]

        def place_of(h):
            lo, hi = h * hd, (h + 1) * hd
            s0, s1 = lo // LANE, -(-hi // LANE)
            w = (s1 - s0) * LANE
            a, b = lo - s0 * LANE, hi - s0 * LANE
            at = 0 if a >= 2 else w - 2
            lane = lax.broadcasted_iota(jnp.int32, (rows, w), 1)
            return lo, hi, s0, s1, w, at, lane, (lane >= a) & (lane < b), slice((s0 - base) * LANE, (s1 - base) * LANE)

        def scores(h):
            _, _, _, _, w, at, _, own, cols = place_of(h)
            q = jnp.where(own, proj[i, 0, :, cols], tags(w, at, 1.0, 0.0))
            k = jnp.where(own, proj[i, 1, :, cols], tags(w, at, 0.0, FAR_BELOW))
            return lax.dot_general(q, k, (((1,), (1,)), ((), ())), preferred_element_type=jnp.float32)

        partial = oc_in[i][...] if later else None
        upcoming = scores(h0)
        for h in range(h0, h1):
            lo, hi, s0, s1, w, at, lane, own, cols = place_of(h)
            s = upcoming
            if h + 1 < h1:
                upcoming = scores(h + 1)
            ones = jnp.where(lane == at, 1.0, 0.0).astype(jnp.bfloat16)
            v = jnp.where(own, proj[i, 2, :, cols], ones)
            m = jnp.max(s, axis=1, keepdims=True) * c
            e = jnp.exp2(s * c - m).astype(jnp.bfloat16)
            o = jnp.dot(e, v, preferred_element_type=jnp.float32)
            o = (o / o[:, at : at + 1]).astype(jnp.bfloat16)
            for t in range(s0, s1):
                piece = o[:, (t - s0) * LANE : (t - s0 + 1) * LANE]
                start = max(lo - t * LANE, 0)
                if start > 0:
                    lanes = lax.broadcasted_iota(jnp.int32, (rows, LANE), 1)
                    piece = jnp.where(lanes < start, partial, piece)
                if hi >= (t + 1) * LANE:
                    j = t - first_tile
                    if last:
                        done[i, :, j * LANE : (j + 1) * LANE] = piece
                    else:
                        done_refs[i][:, j * LANE : (j + 1) * LANE] = piece
                    partial = None
                else:
                    partial = piece
        if last:
            to = out.at[pl.ds(bundle * rows, rows), pl.ds(first_tile * LANE, done.shape[2])]
            copies.append(pltpu.make_async_copy(done.at[i], to, own_sems.at[i]))
            copies[-1].start()
        else:
            oc_out[i][...] = jnp.zeros((rows, LANE), jnp.bfloat16) if partial is None else partial
    for copy in copies:
        copy.wait()


def attend(spans, h0, h1, bundles, xs, ws, info, carry, finished):
    rows, d = xs[0].shape
    hd = d // HEADS
    t0, t1 = spans[0][0], spans[-1][1]
    nb, nt = len(bundles), t1 - t0
    first_tile = h0 * hd // LANE
    tiles = h1 * hd // LANE - first_tile
    last = t1 * LANE == d
    inside = pl.BlockSpec(memory_space=pltpu.VMEM)
    anywhere = pl.BlockSpec(memory_space=pl.ANY)
    scalars = pl.BlockSpec(memory_space=pltpu.SMEM)
    operands = [*xs, *ws, *info]
    specs = [inside] * (nb + len(ws)) + [scalars] * 3
    if t0 > 0:
        operands += [carry[b][0] for b in bundles] + [carry[b][1] for b in bundles]
        specs += [inside] * (2 * nb)
    shape = lambda r, c: jax.ShapeDtypeStruct((r, c), jnp.bfloat16)
    scratch = [pltpu.VMEM((nb, 3, rows, (nt + 1) * LANE), jnp.bfloat16)]
    if last:
        earlier = [(b, tile) for b, tile, _ in finished]
        operands += [x for _, _, x in finished]
        specs += [anywhere] * len(finished)
        out_shape, out_specs = shape(2 * rows, d), anywhere
        scratch += [
            pltpu.VMEM((nb, rows, tiles * LANE), jnp.bfloat16),
            pltpu.SemaphoreType.DMA((len(finished),)),
            pltpu.SemaphoreType.DMA((nb,)),
        ]
    else:
        earlier = None
        out_shape = [shape(rows, tiles * LANE)] * nb + [shape(rows, 3 * LANE)] * nb + [shape(rows, LANE)] * nb
        out_specs = [inside] * (3 * nb)
    res = pl.pallas_call(
        functools.partial(attend_kernel, spans, h0, h1, hd, bundles, earlier),
        out_shape=out_shape,
        in_specs=specs,
        out_specs=out_specs,
        scratch_shapes=scratch,
        compiler_params=pltpu.CompilerParams(vmem_limit_bytes=16 * 2**20),
        name=f"attend_{t0}_{bundles[0]}",
    )(*operands)
    if last:
        return res
    for i, b in enumerate(bundles):
        carry[b] = (res[nb + i], res[2 * nb + i])
        finished.append((b, first_tile, res[i]))
    return res[2 * nb]


ARRIVAL = ((1, 0), (3, 0), (1, 2), (3, 2), (2, 0), (2, 2))


def quarter_of(rank):
    return ((((rank >> 2) ^ (rank >> 1)) & 1) << 1) | (rank & 1)


def source_columns(rank, column, shard_rows, shards):
    quarter = shard_rows // PIECES
    step = np.array([s for core in (0, 1) for s, _ in ARRIVAL for _ in range(quarter)])
    flip = np.array([core | across for core in (0, 1) for _, across in ARRIVAL for _ in range(quarter)])
    row = np.array(list(range(quarter)) * (2 * len(ARRIVAL)))
    rest = ((column - step) % shards) * shard_rows + (quarter_of(rank) ^ flip) * quarter + row
    own = column * shard_rows + np.arange(shard_rows)
    return jnp.concatenate([own, rest]).astype(jnp.int32)


def reordered(x, place):
    return jnp.dot(x, place, preferred_element_type=jnp.float32).astype(jnp.bfloat16)


def shifted(x, axis, by):
    n = lax.axis_size(axis)
    return lax.ppermute(x, axis, [(i, (i + by) % n) for i in range(n)])


def swapped(x, mask):
    n = lax.axis_size("dp")
    return lax.ppermute(x, "dp", [(i, i ^ mask) for i in range(n)])


def fence(*values):
    return lax.optimization_barrier(values)


def stacked(*xs):
    return jnp.concatenate(xs, axis=0)


def on_device(tokens, qkv_weight, image_lengths, balance):
    ranks = lax.axis_size("dp")
    shards = lax.axis_size("fsdp")
    rank = lax.axis_index("dp")
    column = lax.axis_index("fsdp")
    rows, width = tokens.shape
    shard_rows = qkv_weight.shape[0]
    quarter = shard_rows // PIECES
    hd = width // HEADS
    sources = jnp.stack([(rank - 1) % ranks, (rank - ranks // 2) % ranks]).astype(jnp.int32)
    info = (image_lengths, balance, sources)
    columns = source_columns(rank, column, shard_rows, shards)
    quarter_start = quarter_of(rank) * quarter

    def columns_matrix():
        return (jnp.arange(width, dtype=jnp.int32)[:, None] == columns[None, :]).astype(jnp.bfloat16)

    def of_chunk(w, t0, t1):
        return jnp.concatenate([w[:, p * width + t0 * LANE : p * width + t1 * LANE] for p in range(3)], axis=1)

    def payload(w, *chunks):
        own = lax.dynamic_slice_in_dim(w, quarter_start, quarter, 0)
        return jnp.concatenate(fence(*[of_chunk(own, *BOUNDS[c]) for c in chunks]), axis=1)

    def up(x):
        return shifted(x, "fsdp", 1)

    def down(x):
        return shifted(x, "fsdp", shards - 1)

    def across(c, *xs):
        return swapped(stacked(*xs) if len(xs) > 1 else xs[0], SWAPS[c])

    heads = heads_of(BOUNDS, hd)
    carry = [None, None]
    finished = []
    w = qkv_weight
    n_a, n_b, n_c, n_d = [3 * (t1 - t0) * LANE for t0, t1 in BOUNDS]

    pab = payload(w, 0, 1)
    abp, abm = up(pab), down(pab)
    tokens, w, _ = fence(tokens, w, pab)
    near_first = balance[rank, 0, 0] == 0
    low, high = tokens[: rows // 2], tokens[rows // 2 :]
    near_out, far_out = jnp.where(near_first, low, high), jnp.where(near_first, high, low)
    cut = (rows // 5 // 16 * 16, rows * 2 // 7 // 16 * 16)
    far_1 = shifted(far_out[: cut[0]], "dp", ranks // 2)
    near_in = shifted(near_out, "dp", 1)
    pcd = payload(w, 2, 3)

    abp, pcd, w = fence(abp, pcd, w)
    ab2 = up(abp)
    own_a = of_chunk(w, *BOUNDS[0])
    place = columns_matrix()

    abp, abm, pcd, own_a, place, w, far_out = fence(abp, abm, pcd, own_a, place, w, far_out)
    cdp = up(pcd)
    ax = across(0, abp[:, :n_a], abm[:, :n_a])
    far_2 = shifted(far_out[cut[0] : cut[1]], "dp", ranks // 2)
    own_b = of_chunk(w, *BOUNDS[1])

    near, own_b, place = fence(near_in, own_b, place)
    near = reordered(near, place)

    near, ab2, pcd, w = fence(near, ab2, pcd, w)
    cdm = down(pcd)
    ay = across(0, ab2[:, :n_a])
    own_c = of_chunk(w, *BOUNDS[2])

    ax, abp, abm, ab2, own_c, w, far_1 = fence(ax, abp, abm, ab2, own_c, w, far_1)
    bx = across(1, abp[:, n_a:], abm[:, n_a:], ab2[:, n_a:])
    own_d = of_chunk(w, *BOUNDS[3])

    ay, ax, abp, abm, ab2, own_d, cdp, far_out, far_2 = fence(ay, ax, abp, abm, ab2, own_d, cdp, far_out, far_2)
    far_3 = shifted(far_out[cut[1] :], "dp", ranks // 2)
    cd2 = up(cdp)
    both_a = stacked(abp[:, :n_a], abm[:, :n_a], ax, ab2[:, :n_a], ay)
    ac = swapped(both_a, 1)

    ac, both_a, own_a, near, cdm = fence(ac, both_a, own_a, near, cdm)
    wa = stacked(own_a, both_a, ac)
    out = attend(BOUNDS[:1], *heads[0], (0,), (near,), (wa,), info, carry, finished)

    out, cdp, cdm, far_1, far_2, far_3 = fence(out, cdp, cdm, far_1, far_2, far_3)
    dx_1 = across(3, cdp[:, n_c:], cdm[:, n_c:])
    cx_1 = across(2, cdp[:, :n_c], cdm[:, :n_c])
    far = reordered(stacked(far_1, far_2, far_3), place)

    bx, far, cd2 = fence(bx, far, cd2)
    dx_2 = across(3, cd2[:, n_c:])
    cx_2 = across(2, cd2[:, :n_c])
    both_b = stacked(abp[:, n_a:], abm[:, n_a:], bx[: 2 * quarter], ab2[:, n_a:], bx[2 * quarter :])
    bc = swapped(both_b, 1)
    out = attend(BOUNDS[:1], *heads[0], (1,), (far,), (wa,), info, carry, finished)

    out, bc, both_b, own_b, cx_1, dx_1, cdp = fence(out, bc, both_b, own_b, cx_1, dx_1, cdp)
    wb = stacked(own_b, both_b, bc)
    out = attend(BOUNDS[1:2], *heads[1], (0,), (near,), (wb,), info, carry, finished)

    out, cx_1, dx_1, cx_2, dx_2, cdp, cdm, cd2 = fence(out, cx_1, dx_1, cx_2, dx_2, cdp, cdm, cd2)
    both_c = stacked(cdp[:, :n_c], cdm[:, :n_c], cx_1, cd2[:, :n_c], cx_2)
    cc = swapped(both_c, 1)
    both_d = stacked(cdp[:, n_c:], cdm[:, n_c:], dx_1, cd2[:, n_c:], dx_2)
    dc = swapped(both_d, 1)
    out = attend(BOUNDS[1:2], *heads[1], (1,), (far,), (wb,), info, carry, finished)

    wc = stacked(own_c, both_c, cc)
    wd = stacked(own_d, both_d, dc)
    return attend(BOUNDS[2:], heads[2][0], heads[3][1], (0, 1), (near, far), (wc, wd), info, carry, finished)


def solution(mesh):
    in_specs = (
        P(("dp", "fsdp"), None),
        P("fsdp", None),
        P(None, "fsdp", None, None),
        P(None, "fsdp", None),
    )
    return jax.shard_map(
        on_device, mesh=mesh, in_specs=in_specs, out_specs=P(("dp", "fsdp"), None), check_vma=False
    )
```

```python
import functools
import math

import jax
import jax.numpy as jnp
import numpy as np
from jax import lax
from jax.experimental import pallas as pl
from jax.experimental.pallas import tpu as pltpu
from jax.sharding import PartitionSpec as P

HEADS = 16
LANE = 128
FAR_BELOW = -1e30
PIECES = 4
BOUNDS = ((0, 3), (3, 6), (6, 9), (9, 11))
SWAPS = (2, 2, 2, 4)


def heads_of(bounds, head_dim):
    found, h = [], 0
    for _, t1 in bounds:
        end = min(HEADS, t1 * LANE // head_dim)
        found.append((h, end))
        h = end
    return found


def pick_kernel(route_ref, rank_ref, tokens, near, far, sems):
    rows = near.shape[0]
    copies = []
    for r, to in enumerate((near, far)):
        start = pl.multiple_of(route_ref[rank_ref[0], 0, r] * rows, rows)
        copies.append(pltpu.make_async_copy(tokens.at[pl.ds(start, rows)], to, sems.at[r]))
    for c in copies:
        c.start()
    for c in copies:
        c.wait()


def picked(balance, rank, tokens):
    rows, width = tokens.shape
    anywhere = pl.BlockSpec(memory_space=pl.ANY)
    scalars = pl.BlockSpec(memory_space=pltpu.SMEM)
    half = jax.ShapeDtypeStruct((rows // 2, width), tokens.dtype)
    return pl.pallas_call(
        pick_kernel,
        out_shape=[half, half],
        in_specs=[scalars, scalars, anywhere],
        out_specs=[pl.BlockSpec(memory_space=pltpu.VMEM)] * 2,
        scratch_shapes=[pltpu.SemaphoreType.DMA((2,))],
        name="pick",
    )(balance, rank, tokens)


def attend_kernel(spans, h0, h1, hd, bundles, earlier, *refs):
    nb = len(bundles)
    refs = list(refs)
    take = lambda n: [refs.pop(0) for _ in range(n)]
    x_refs, w_refs = take(nb), take(len(spans))
    lengths_ref, route_ref, source_ref = take(3)
    t0, t1 = spans[0][0], spans[-1][1]
    later = t0 > 0
    pc_in, oc_in = (take(nb), take(nb)) if later else (None, None)
    last = earlier is not None
    if last:
        before = take(len(earlier))
        out = refs.pop(0)
        proj, done, sems, own_sems = refs
    else:
        done_refs, pc_out, oc_out = take(nb), take(nb), take(nb)
        (proj,) = refs
    rows = x_refs[0].shape[0]
    nt = t1 - t0
    base = t0 - 1
    first_tile = h0 * hd // LANE
    c = math.log2(math.e) / math.sqrt(hd)
    copies = []
    if last:
        for j, (bundle, tile) in enumerate(earlier):
            to = out.at[pl.ds(bundle * rows, rows), pl.ds(tile * LANE, before[j].shape[1])]
            copies.append(pltpu.make_async_copy(before[j], to, sems.at[j]))
            copies[-1].start()
    for i, bundle in enumerate(bundles):
        for w_ref, (u0, u1) in zip(w_refs, spans):
            p = jnp.dot(x_refs[i][...], w_ref[...], preferred_element_type=jnp.float32).astype(jnp.bfloat16)
            n = (u1 - u0) * LANE
            for part in range(3):
                proj[i, part, :, (u0 - base) * LANE : (u1 - base) * LANE] = p[:, part * n : (part + 1) * n]
        for part in range(3):
            if later:
                proj[i, part, :, :LANE] = pc_in[i][:, part * LANE : (part + 1) * LANE]
            if not last:
                pc_out[i][:, part * LANE : (part + 1) * LANE] = proj[i, part, :, nt * LANE :]
        source = source_ref[bundle]
        split = lengths_ref[source, 0, route_ref[source, 0, bundle], 0]
        made = {}

        def tags(w, at, a, b):
            if (w, at, a, b) not in made:
                late = lax.broadcasted_iota(jnp.int32, (rows, w), 0) >= split
                lane = lax.broadcasted_iota(jnp.int32, (rows, w), 1)
                one, two = jnp.where(late, b, a), jnp.where(late, a, b)
                both = jnp.where(lane == at, one, jnp.where(lane == at + 1, two, 0.0))
                made[(w, at, a, b)] = both.astype(jnp.bfloat16)
            return made[(w, at, a, b)]

        def place_of(h):
            lo, hi = h * hd, (h + 1) * hd
            s0, s1 = lo // LANE, -(-hi // LANE)
            w = (s1 - s0) * LANE
            a, b = lo - s0 * LANE, hi - s0 * LANE
            at = 0 if a >= 2 else w - 2
            lane = lax.broadcasted_iota(jnp.int32, (rows, w), 1)
            return lo, hi, s0, s1, w, at, lane, (lane >= a) & (lane < b), slice((s0 - base) * LANE, (s1 - base) * LANE)

        def scores(h):
            _, _, _, _, w, at, _, own, cols = place_of(h)
            q = jnp.where(own, proj[i, 0, :, cols], tags(w, at, 1.0, 0.0))
            k = jnp.where(own, proj[i, 1, :, cols], tags(w, at, 0.0, FAR_BELOW))
            return lax.dot_general(q, k, (((1,), (1,)), ((), ())), preferred_element_type=jnp.float32)

        partial = oc_in[i][...] if later else None
        upcoming = scores(h0)
        for h in range(h0, h1):
            lo, hi, s0, s1, w, at, lane, own, cols = place_of(h)
            s = upcoming
            if h + 1 < h1:
                upcoming = scores(h + 1)
            ones = jnp.where(lane == at, 1.0, 0.0).astype(jnp.bfloat16)
            v = jnp.where(own, proj[i, 2, :, cols], ones)
            m = jnp.max(s, axis=1, keepdims=True) * c
            e = jnp.exp2(s * c - m).astype(jnp.bfloat16)
            o = jnp.dot(e, v, preferred_element_type=jnp.float32)
            o = (o / o[:, at : at + 1]).astype(jnp.bfloat16)
            for t in range(s0, s1):
                piece = o[:, (t - s0) * LANE : (t - s0 + 1) * LANE]
                start = max(lo - t * LANE, 0)
                if start > 0:
                    lanes = lax.broadcasted_iota(jnp.int32, (rows, LANE), 1)
                    piece = jnp.where(lanes < start, partial, piece)
                if hi >= (t + 1) * LANE:
                    j = t - first_tile
                    if last:
                        done[i, :, j * LANE : (j + 1) * LANE] = piece
                    else:
                        done_refs[i][:, j * LANE : (j + 1) * LANE] = piece
                    partial = None
                else:
                    partial = piece
        if last:
            to = out.at[pl.ds(bundle * rows, rows), pl.ds(first_tile * LANE, done.shape[2])]
            copies.append(pltpu.make_async_copy(done.at[i], to, own_sems.at[i]))
            copies[-1].start()
        else:
            oc_out[i][...] = jnp.zeros((rows, LANE), jnp.bfloat16) if partial is None else partial
    for copy in copies:
        copy.wait()


def attend(spans, h0, h1, bundles, xs, ws, info, carry, finished):
    rows, d = xs[0].shape
    hd = d // HEADS
    t0, t1 = spans[0][0], spans[-1][1]
    nb, nt = len(bundles), t1 - t0
    first_tile = h0 * hd // LANE
    tiles = h1 * hd // LANE - first_tile
    last = t1 * LANE == d
    inside = pl.BlockSpec(memory_space=pltpu.VMEM)
    anywhere = pl.BlockSpec(memory_space=pl.ANY)
    scalars = pl.BlockSpec(memory_space=pltpu.SMEM)
    operands = [*xs, *ws, *info]
    specs = [inside] * (nb + len(ws)) + [scalars] * 3
    if t0 > 0:
        operands += [carry[b][0] for b in bundles] + [carry[b][1] for b in bundles]
        specs += [inside] * (2 * nb)
    shape = lambda r, c: jax.ShapeDtypeStruct((r, c), jnp.bfloat16)
    scratch = [pltpu.VMEM((nb, 3, rows, (nt + 1) * LANE), jnp.bfloat16)]
    if last:
        earlier = [(b, tile) for b, tile, _ in finished]
        operands += [x for _, _, x in finished]
        specs += [anywhere] * len(finished)
        out_shape, out_specs = shape(2 * rows, d), anywhere
        scratch += [
            pltpu.VMEM((nb, rows, tiles * LANE), jnp.bfloat16),
            pltpu.SemaphoreType.DMA((len(finished),)),
            pltpu.SemaphoreType.DMA((nb,)),
        ]
    else:
        earlier = None
        out_shape = [shape(rows, tiles * LANE)] * nb + [shape(rows, 3 * LANE)] * nb + [shape(rows, LANE)] * nb
        out_specs = [inside] * (3 * nb)
    res = pl.pallas_call(
        functools.partial(attend_kernel, spans, h0, h1, hd, bundles, earlier),
        out_shape=out_shape,
        in_specs=specs,
        out_specs=out_specs,
        scratch_shapes=scratch,
        compiler_params=pltpu.CompilerParams(vmem_limit_bytes=16 * 2**20),
        name=f"attend_{t0}_{bundles[0]}",
    )(*operands)
    if last:
        return res
    for i, b in enumerate(bundles):
        carry[b] = (res[nb + i], res[2 * nb + i])
        finished.append((b, first_tile, res[i]))
    return res[2 * nb]


ARRIVAL = ((1, 0), (3, 0), (1, 2), (3, 2), (2, 0), (2, 2))


def quarter_of(rank):
    return ((((rank >> 2) ^ (rank >> 1)) & 1) << 1) | (rank & 1)


def source_columns(rank, column, shard_rows, shards):
    quarter = shard_rows // PIECES
    step = np.array([s for core in (0, 1) for s, _ in ARRIVAL for _ in range(quarter)])
    flip = np.array([core | across for core in (0, 1) for _, across in ARRIVAL for _ in range(quarter)])
    row = np.array(list(range(quarter)) * (2 * len(ARRIVAL)))
    rest = ((column - step) % shards) * shard_rows + (quarter_of(rank) ^ flip) * quarter + row
    own = column * shard_rows + np.arange(shard_rows)
    return jnp.concatenate([own, rest]).astype(jnp.int32)


def reordered(x, place):
    return jnp.dot(x, place, preferred_element_type=jnp.float32).astype(jnp.bfloat16)


def shifted(x, axis, by):
    n = lax.axis_size(axis)
    return lax.ppermute(x, axis, [(i, (i + by) % n) for i in range(n)])


def swapped(x, mask):
    n = lax.axis_size("dp")
    return lax.ppermute(x, "dp", [(i, i ^ mask) for i in range(n)])


def fence(*values):
    return lax.optimization_barrier(values)


def stacked(*xs):
    return jnp.concatenate(xs, axis=0)


def on_device(tokens, qkv_weight, image_lengths, balance):
    ranks = lax.axis_size("dp")
    shards = lax.axis_size("fsdp")
    rank = lax.axis_index("dp")
    column = lax.axis_index("fsdp")
    rows, width = tokens.shape
    shard_rows = qkv_weight.shape[0]
    quarter = shard_rows // PIECES
    hd = width // HEADS
    sources = jnp.stack([(rank - 1) % ranks, (rank - ranks // 2) % ranks]).astype(jnp.int32)
    info = (image_lengths, balance, sources)
    columns = source_columns(rank, column, shard_rows, shards)
    quarter_start = quarter_of(rank) * quarter

    def columns_matrix():
        return (jnp.arange(width, dtype=jnp.int32)[:, None] == columns[None, :]).astype(jnp.bfloat16)

    def of_chunk(w, t0, t1):
        return jnp.concatenate([w[:, p * width + t0 * LANE : p * width + t1 * LANE] for p in range(3)], axis=1)

    def payload(w, *chunks):
        own = lax.dynamic_slice_in_dim(w, quarter_start, quarter, 0)
        return jnp.concatenate(fence(*[of_chunk(own, *BOUNDS[c]) for c in chunks]), axis=1)

    def up(x):
        return shifted(x, "fsdp", 1)

    def down(x):
        return shifted(x, "fsdp", shards - 1)

    def across(c, *xs):
        return swapped(stacked(*xs) if len(xs) > 1 else xs[0], SWAPS[c])

    heads = heads_of(BOUNDS, hd)
    carry = [None, None]
    finished = []
    w = qkv_weight
    n_a, n_b, n_c, n_d = [3 * (t1 - t0) * LANE for t0, t1 in BOUNDS]

    pab = payload(w, 0, 1)
    abp, abm = up(pab), down(pab)
    tokens, w, _ = fence(tokens, w, pab)
    near_first = balance[rank, 0, 0] == 0
    low, high = tokens[: rows // 2], tokens[rows // 2 :]
    near_out, far_out = jnp.where(near_first, low, high), jnp.where(near_first, high, low)
    cut = (rows // 5 // 16 * 16, rows * 2 // 7 // 16 * 16, rows * 7 // 20 // 16 * 16)
    far_1 = shifted(far_out[: cut[0]], "dp", ranks // 2)
    near_in = shifted(near_out, "dp", 1)
    pcd = payload(w, 2, 3)

    abp, pcd, w = fence(abp, pcd, w)
    ab2 = up(abp)
    own_a = of_chunk(w, *BOUNDS[0])
    place = columns_matrix()

    abp, abm, pcd, own_a, place, w, far_out = fence(abp, abm, pcd, own_a, place, w, far_out)
    cdp = up(pcd)
    ax = across(0, abp[:, :n_a], abm[:, :n_a])
    far_2 = shifted(far_out[cut[0] : cut[1]], "dp", ranks // 2)
    own_b = of_chunk(w, *BOUNDS[1])

    near, own_b, place = fence(near_in, own_b, place)
    near = reordered(near, place)

    near, ab2, pcd, w = fence(near, ab2, pcd, w)
    cdm = down(pcd)
    ay = across(0, ab2[:, :n_a])
    own_c = of_chunk(w, *BOUNDS[2])

    ax, abp, abm, ab2, own_c, w, far_1 = fence(ax, abp, abm, ab2, own_c, w, far_1)
    bx = across(1, abp[:, n_a:], abm[:, n_a:], ab2[:, n_a:])
    own_d = of_chunk(w, *BOUNDS[3])

    ay, ax, abp, abm, ab2, own_d, cdp, far_out, far_2 = fence(ay, ax, abp, abm, ab2, own_d, cdp, far_out, far_2)
    far_3 = shifted(far_out[cut[1] : cut[2]], "dp", ranks // 2)
    cd2 = up(cdp)
    both_a = stacked(abp[:, :n_a], abm[:, :n_a], ax, ab2[:, :n_a], ay)
    ac = swapped(both_a, 1)

    ac, both_a, own_a, near, far_3, far_out = fence(ac, both_a, own_a, near, far_3, far_out)
    far_4 = shifted(far_out[cut[2] :], "dp", ranks // 2)
    wa = stacked(own_a, both_a, ac)
    out = attend(BOUNDS[:1], *heads[0], (0,), (near,), (wa,), info, carry, finished)

    out, cdp, cdm, far_1, far_2, far_3, far_4 = fence(out, cdp, cdm, far_1, far_2, far_3, far_4)
    dx_1 = across(3, cdp[:, n_c:], cdm[:, n_c:])
    cx_1 = across(2, cdp[:, :n_c], cdm[:, :n_c])
    far = reordered(stacked(far_1, far_2, far_3, far_4), place)

    bx, far, cd2 = fence(bx, far, cd2)
    dx_2 = across(3, cd2[:, n_c:])
    cx_2 = across(2, cd2[:, :n_c])
    both_b = stacked(abp[:, n_a:], abm[:, n_a:], bx[: 2 * quarter], ab2[:, n_a:], bx[2 * quarter :])
    bc = swapped(both_b, 1)
    out = attend(BOUNDS[:1], *heads[0], (1,), (far,), (wa,), info, carry, finished)

    out, bc, both_b, own_b, cx_1, dx_1, cdp = fence(out, bc, both_b, own_b, cx_1, dx_1, cdp)
    wb = stacked(own_b, both_b, bc)
    out = attend(BOUNDS[1:2], *heads[1], (0,), (near,), (wb,), info, carry, finished)

    out, cx_1, dx_1, cx_2, dx_2, cdp, cdm, cd2 = fence(out, cx_1, dx_1, cx_2, dx_2, cdp, cdm, cd2)
    both_c = stacked(cdp[:, :n_c], cdm[:, :n_c], cx_1, cd2[:, :n_c], cx_2)
    cc = swapped(both_c, 1)
    both_d = stacked(cdp[:, n_c:], cdm[:, n_c:], dx_1, cd2[:, n_c:], dx_2)
    dc = swapped(both_d, 1)
    out = attend(BOUNDS[1:2], *heads[1], (1,), (far,), (wb,), info, carry, finished)

    wc = stacked(own_c, both_c, cc)
    wd = stacked(own_d, both_d, dc)
    return attend(BOUNDS[2:], heads[2][0], heads[3][1], (0, 1), (near, far), (wc, wd), info, carry, finished)


def solution(mesh):
    in_specs = (
        P(("dp", "fsdp"), None),
        P("fsdp", None),
        P(None, "fsdp", None, None),
        P(None, "fsdp", None),
    )
    return jax.shard_map(
        on_device, mesh=mesh, in_specs=in_specs, out_specs=P(("dp", "fsdp"), None), check_vma=False
    )
```
